128 devices in a mesh: aux: 16 (over x, z), orb: 8 (over y, core).
Axes of the slice: x: 4, y: 4, z: 4, core: 2. Of those that a mesh axis runs over, the one named last changes fastest.
Arguments:
- integrals: bfloat16 [32, 128, 8, 128, 128], P('aux', 'orb'), may hold values from -0.1875 to 0.1875
- panels: bfloat16 [8, 128, 1920], P('orb'), may hold values from -6 to 6
- screen: int32 [16, 128, 8], replicated, may hold values from 0 to 1, as said below
- owner_map: int32 [8], replicated, may hold values from 0 to 7, each once
Outputs:
- halves: bfloat16 [128, 32, 128, 1920], P(('orb', 'aux'))
- kblocks: float32 [128, 128, 128], P(('orb', 'aux'))
The draws below stay inside these ranges and needn't reach their ends.
Inputs may be any that keep to these rules, and one draw needn't show every extreme that they name: `screen`: 1 where the block of an auxiliary tile, an orbital row block and a panel survives screening, 0 where it is screened out; the kept share differs from row block to row block. A permutation: panel j is stored at position owner_map[j] of panels.
All inputs are finite; a program needn't handle non-finite values.
Results may differ from the reference program's by a relative error of at most 0.001.
Values may be sent and summed in bfloat16 or wider, within the bound.
A program may use at most 128 MiB of HBM per device.

```python
import jax
import jax.numpy as jnp
from jax import lax

BS = 128
NLB = 8
ATILE = 2
NOCC = 1920
NAUX = 32
NAT = 16
NRB = 128


def draw_screen(key, part):
    key = jax.random.fold_in(key, 11)
    first_key, second_key = jax.random.split(key)
    level = jax.random.randint(first_key, (1, NRB, 1), 25, 101)
    score = jax.random.randint(second_key, (NAT, NRB, NLB), 0, 100)
    return (score < level).astype(jnp.int32)


def block_levels(key, shape, shards, low, largest):
    def one(dim, shards_of):
        heights = jax.random.uniform(jax.random.fold_in(jax.random.fold_in(key, 6), dim), (shards_of,), jnp.float32, low / len(shards), largest / len(shards))
        return jnp.repeat(jnp.exp(heights), shape[dim] // shards_of).reshape((-1,) + (1,) * (len(shape) - dim - 1))

    level = one(*shards[0])
    for cut in shards[1:]:
        level = level * one(*cut)
    return level


def gaussian(own_key, dims, spread, most, shards=(), kind=jnp.bfloat16):
    result = spread * jax.random.normal(own_key, dims, jnp.float32)
    if shards:
        result = result * block_levels(own_key, dims, shards, -0.22, 0.18)
    return jnp.clip(result, -most, most).astype(kind)


def setup_inputs(seed: int = 0) -> dict:
    streams_of = jax.random.split(jax.random.key(seed), 5)
    integrals = gaussian(streams_of[0], (NAUX, NRB, NLB, BS, BS), (NLB * BS) ** -0.5, 0.1875, ((0, 16), (1, 8)))
    panels = gaussian(streams_of[1], (NLB, BS, NOCC), 1.0, 6.0, ((0, 8),))
    screen = draw_screen(jax.random.fold_in(streams_of[4], 71), 0)
    owner_map = jax.random.permutation(streams_of[3], NLB).astype(jnp.int32)
    return {"integrals": integrals, "panels": panels, "screen": screen, "owner_map": owner_map}


def reference(integrals, panels, screen, owner_map):
    density = jnp.take(panels, owner_map, axis=0)
    density_wide = density.astype(jnp.float32)
    keep_mask = jnp.repeat(screen, ATILE, axis=0).astype(jnp.bfloat16)
    norm_factor = 1.0 / (NAUX * NOCC)

    def row_block(row_index):
        tile_rows = lax.dynamic_index_in_dim(integrals, row_index, 1, keepdims=False)
        keep_row = lax.dynamic_index_in_dim(keep_mask, row_index, 1, keepdims=False)
        masked = (tile_rows * keep_row[:, :, None, None]).astype(jnp.float32)
        product = jnp.einsum("pjib,jbo->pio", masked, density_wide)
        rounded = product.astype(jnp.bfloat16)
        half_wide = rounded.astype(jnp.float32)
        gram = jnp.einsum("pio,pko->ik", half_wide, half_wide) * norm_factor
        return rounded, gram

    halves, kblocks = lax.map(row_block, jnp.arange(NRB, dtype=jnp.int32))
    return halves, kblocks
```

```python
import functools

import jax
import jax.numpy as jnp
from jax import lax
from jax.experimental import pallas as pl
from jax.experimental.pallas import tpu as pltpu
from jax.sharding import PartitionSpec as P

MESH = pl.DeviceIdType.MESH
BS = 128
NLB = 8
NOCC = 1920
NAUX = 32
NAT = 16
NRB = 128
DEPTH = NLB * BS
SIDE = 4
SCALE = 1.0 / (NAUX * NOCC)
ORDER = (2, 3, 1)
COLUMNS = ((0, 512), (512, 512), (1024, 512), (1536, 384))
EARLY = [(0, 0)] + [(d, 0) for d in ORDER] + [(0, e) for e in ORDER] + [(d, 2) for d in ORDER] + [(2, 3), (2, 1), (3, 3), (3, 1)]
LATE = [(1, 3), (1, 1)]


def place():
    a, o = lax.axis_index("aux"), lax.axis_index("orb")
    return a // SIDE, a % SIDE, o // 2, o % 2


def tile_of(x, z, dx, dz):
    return (x + SIDE - dx) % SIDE * SIDE + (z + SIDE - dz) % SIDE


def transform(x, z, d, e, fin_ref, mask_ref, dens_ref, lhs, put):
    for p, (dx, dz) in ((0, (d, e)), (1, (e, d))):
        keep = mask_ref[pl.ds(tile_of(x, z, dx, dz), 1), :]
        for j in range(NLB):
            block = fin_ref[p, dx, dz, j].astype(jnp.float32) * keep[:, j * BS : (j + 1) * BS]
            lhs[p * BS : (p + 1) * BS, j * BS : (j + 1) * BS] = block.astype(jnp.bfloat16)
    for at, width in COLUMNS:
        product = jnp.dot(lhs[...], dens_ref[:, at : at + width], preferred_element_type=jnp.float32)
        put(at, width, product.astype(jnp.bfloat16))


def gram(half):
    return lax.dot_general(half, half, (((1,), (1,)), ((), ())), preferred_element_type=jnp.float32)


def gather_kernel(
    ints, panel, screen, owner, hv, fin, dens, mask, kacc,
    xa, zb, prcv, scr, own, lhs, s_one, r_one, s_two, r_fin, s_pan, r_pan, l_sem,
):
    x, z, y, c = place()
    o = y * 2 + c

    def at_xz(dx, dz):
        return ((x + dx) % SIDE * SIDE + (z + dz) % SIDE, o)

    def at_orb(dy, dc):
        return (x * SIDE + z, (y + dy) % SIDE * 2 + (c + dc) % 2)

    def send(src, dst, ss, rs, to):
        return pltpu.make_async_remote_copy(
            src_ref=src, dst_ref=dst, send_sem=ss, recv_sem=rs, device_id=to, device_id_type=MESH
        )

    barrier = pltpu.get_barrier_semaphore()
    for d in (1, 2, 3):
        for to in (at_xz(d, 0), at_xz(0, d), at_orb(d, 0)):
            pl.semaphore_signal(barrier, inc=1, device_id=to, device_id_type=MESH)
    pl.semaphore_signal(barrier, inc=1, device_id=at_orb(0, 1), device_id_type=MESH)
    pl.semaphore_wait(barrier, 10)

    relay_a, relay_b = {}, {}
    for d in ORDER:
        for e in ORDER:
            relay_a[d, e] = send(ints.at[0, (x + d) % SIDE, (z + e) % SIDE], xa.at[d - 1, e - 1], s_one.at[0, d, e], r_one.at[0, d, e], at_xz(d, 0))
            relay_b[d, e] = send(ints.at[1, (x + e) % SIDE, (z + d) % SIDE], zb.at[d - 1, e - 1], s_one.at[1, d, e], r_one.at[1, d, e], at_xz(0, d))
            relay_a[d, e].start()
            relay_b[d, e].start()
    panels = {d: send(panel.at[0], prcv.at[o], s_pan.at[0, d], r_pan.at[0, d], at_orb(d, 0)) for d in ORDER}
    for d in ORDER:
        panels[d].start()
    direct = []
    for d in ORDER:
        direct.append(send(ints.at[0, (x + d) % SIDE, z], fin.at[0, d, 0], s_one.at[0, d, 0], r_fin.at[0, d, 0], at_xz(d, 0)))
        direct.append(send(ints.at[1, x, (z + d) % SIDE], fin.at[1, 0, d], s_one.at[1, d, 0], r_fin.at[1, d, 0], at_xz(0, d)))
    for e in ORDER:
        direct.append(send(ints.at[0, x, (z + e) % SIDE], fin.at[0, 0, e], s_two.at[0, 0, e], r_fin.at[0, 0, e], at_xz(0, e)))
        direct.append(send(ints.at[1, (x + e) % SIDE, z], fin.at[1, e, 0], s_two.at[1, 0, e], r_fin.at[1, 0, e], at_xz(e, 0)))
    for copy in direct:
        copy.start()
    mine = [
        pltpu.make_async_copy(ints.at[0, x, z], fin.at[0, 0, 0], l_sem.at[0]),
        pltpu.make_async_copy(ints.at[1, x, z], fin.at[1, 0, 0], l_sem.at[1]),
        pltpu.make_async_copy(panel.at[0], prcv.at[o], l_sem.at[2]),
    ]
    row = o * SIDE * SIDE + x * SIDE + z
    masks = pltpu.make_async_copy(screen, scr, l_sem.at[3])
    masks.start()
    owners = pltpu.make_async_copy(owner, own, l_sem.at[4])
    owners.start()
    for copy in mine:
        copy.start()
    shared = {0: send(panel.at[0], prcv.at[o], s_pan.at[1, 0], r_pan.at[1, 0], at_orb(0, 1))}
    shared[0].start()

    masks.wait()
    pick = lax.broadcasted_iota(jnp.int32, (NAT, NLB, NRB), 2) == row
    kept = jnp.sum(jnp.where(pick, scr[...], 0).astype(jnp.float32), axis=2)
    wide = lax.broadcasted_iota(jnp.int32, (NLB, DEPTH), 1) // BS == lax.broadcasted_iota(jnp.int32, (NLB, DEPTH), 0)
    mask[...] = jnp.dot(kept, wide.astype(jnp.float32), preferred_element_type=jnp.float32)
    kacc[...] = jnp.zeros_like(kacc)

    for d in ORDER:
        panels[d].wait_recv()
        slot = (y + SIDE - d) % SIDE * 2 + c
        shared[d] = send(prcv.at[slot], prcv.at[slot], s_pan.at[1, d], r_pan.at[1, d], at_orb(0, 1))
        shared[d].start()

    second = {}
    for d in ORDER:
        for e in ORDER:
            second[0, d, e] = send(xa.at[d - 1, e - 1], fin.at[0, d, e], s_two.at[0, d, e], r_fin.at[0, d, e], at_xz(0, e))
            second[1, d, e] = send(zb.at[d - 1, e - 1], fin.at[1, e, d], s_two.at[1, d, e], r_fin.at[1, d, e], at_xz(e, 0))
    for d in ORDER:
        for e in ORDER:
            relay_a[d, e].wait_recv()
            second[0, d, e].start()
            relay_b[d, e].wait_recv()
            second[1, d, e].start()

    for d in range(SIDE):
        shared[d].wait_recv()
    mine[2].wait()
    owners.wait()
    for j in range(NLB):
        dens[j * BS : (j + 1) * BS, :] = prcv[own[j]]

    def pair(d, e):
        for p, (dx, dz) in ((0, (d, e)), (1, (e, d))):
            send(fin.at[p, dx, dz], fin.at[p, dx, dz], s_one.at[0, 0, 0], r_fin.at[p, d, e], at_xz(1, 0)).wait_recv()

    def work(d, e):
        spots = [tile_of(x, z, d, e) * 2, tile_of(x, z, e, d) * 2 + 1]

        def put(at, width, value):
            for p in range(2):
                hv[pl.ds(spots[p], 1), :, at : at + width] = value[p * BS : (p + 1) * BS].reshape(1, BS, width)

        transform(x, z, d, e, fin, mask, dens, lhs, put)
        for p in range(2):
            kacc[...] += gram(hv[pl.ds(spots[p], 1)].reshape(BS, NOCC))

    mine[0].wait()
    mine[1].wait()
    work(0, 0)

    def step(g, _):
        d, e = pairs(g)
        pair(d, e)
        work(d, e)
        return 0

    lax.fori_loop(0, len(EARLY) - 1, step, 0)
    for d, e in LATE:
        pair(d, e)
    for copy in list(relay_a.values()) + list(relay_b.values()) + direct + list(second.values()) + list(panels.values()) + list(shared.values()):
        copy.wait_send()


def pairs(g):
    first, second, third = g // 3 == 0, g // 3 == 1, g // 3 == 2
    turn = (g + 1) % 3 + 1
    late = g - 9
    d = jnp.where(first | third, turn, jnp.where(second, 0, (late // 2 + 1) % 3 + 1))
    e = jnp.where(first, 0, jnp.where(second, turn, jnp.where(third, 2, 3 - late % 2 * 2)))
    return d, e


def finish_kernel(hv, fin, dens, mask, kacc, halves, kblocks, lhs, late, sems):
    x, z, y, c = place()

    def out(source, spot):
        return pltpu.make_async_copy(source, halves.at[0, spot], sems.at[spot])

    copies = []
    for d, e in EARLY:
        for p, (dx, dz) in ((0, (d, e)), (1, (e, d))):
            spot = tile_of(x, z, dx, dz) * 2 + p
            copies.append(out(hv.at[spot], spot))
            copies[-1].start()
    total = kacc[...]
    for k, (d, e) in enumerate(LATE):

        def put(at, width, value):
            for p in range(2):
                late[2 * k + p, :, at : at + width] = value[p * BS : (p + 1) * BS]

        transform(x, z, d, e, fin, mask, dens, lhs, put)
        for p, (dx, dz) in ((0, (d, e)), (1, (e, d))):
            spot = tile_of(x, z, dx, dz) * 2 + p
            copies.append(out(late.at[2 * k + p], spot))
            copies[-1].start()
            total += gram(late[2 * k + p])
    kblocks[0] = total * SCALE
    for copy in copies:
        copy.wait()


def shards(integrals, panels, screen, owner_map):
    piece = (NLB, BS, BS)
    vmem = pl.BlockSpec(memory_space=pltpu.VMEM)
    hbm = pl.BlockSpec(memory_space=pl.ANY)
    dma = pltpu.SemaphoreType.DMA
    bf16, f32 = jnp.bfloat16, jnp.float32
    ints = integrals.reshape((2, SIDE, SIDE) + piece)
    between = pl.pallas_call(
        gather_kernel,
        name="gather",
        out_shape=[
            pltpu.VMEM((NAUX, BS, NOCC), bf16),
            pltpu.VMEM((2, SIDE, SIDE) + piece, bf16),
            pltpu.VMEM((DEPTH, NOCC), bf16),
            pltpu.VMEM((NAT, DEPTH), f32),
            pltpu.VMEM((BS, BS), f32),
        ],
        in_specs=[hbm] * 4,
        out_specs=[vmem] * 5,
        scratch_shapes=[
            pltpu.VMEM((3, 3) + piece, bf16),
            pltpu.VMEM((3, 3) + piece, bf16),
            pltpu.VMEM((NLB, BS, NOCC), bf16),
            pltpu.VMEM((NAT, NLB, NRB), jnp.int32),
            pltpu.SMEM((NLB,), jnp.int32),
            pltpu.VMEM((2 * BS, DEPTH), bf16),
            dma((2, 4, 4)),
            dma((2, 4, 4)),
            dma((2, 4, 4)),
            dma((2, 4, 4)),
            dma((2, 4)),
            dma((2, 4)),
            dma((5,)),
        ],
        compiler_params=pltpu.CompilerParams(collective_id=0, has_side_effects=True, vmem_limit_bytes=24 << 20),
        cost_estimate=pl.CostEstimate(flops=16 << 30, bytes_accessed=24 << 20, transcendentals=0),
    )(*(pltpu.with_memory_space_constraint(v, pltpu.HBM) for v in (ints, panels, screen.transpose(0, 2, 1), owner_map)))
    return pl.pallas_call(
        finish_kernel,
        name="finish",
        out_shape=[
            jax.ShapeDtypeStruct((1, NAUX, BS, NOCC), bf16),
            jax.ShapeDtypeStruct((1, BS, BS), f32),
        ],
        in_specs=[vmem] * 5,
        out_specs=[hbm, vmem],
        scratch_shapes=[
            pltpu.VMEM((2 * BS, DEPTH), bf16),
            pltpu.VMEM((2 * len(LATE), BS, NOCC), bf16),
            dma((NAUX,)),
        ],
        compiler_params=pltpu.CompilerParams(vmem_limit_bytes=24 << 20),
        cost_estimate=pl.CostEstimate(flops=2 << 30, bytes_accessed=16 << 20, transcendentals=0),
    )(*(pltpu.with_memory_space_constraint(v, pltpu.VMEM) for v in between))


def solution(mesh):
    placed = (P("aux", "orb", None, None, None), P("orb", None, None), P(), P())
    return jax.shard_map(
        shards,
        mesh=mesh,
        in_specs=placed,
        out_specs=(P(("orb", "aux"), None, None, None), P(("orb", "aux"), None, None)),
        check_vma=False,
    )
```

```python
import functools

import jax
import jax.numpy as jnp
from jax import lax
from jax.experimental import pallas as pl
from jax.experimental.pallas import tpu as pltpu
from jax.sharding import PartitionSpec as P

MESH = pl.DeviceIdType.MESH
BS = 128
NLB = 8
NOCC = 1920
NAUX = 32
NAT = 16
NRB = 128
DEPTH = NLB * BS
SIDE = 4
SCALE = 1.0 / (NAUX * NOCC)
ORDER = (2, 3, 1)
STEP = 640
COLUMNS = ((0, 512), (512, 512), (1024, 512), (1536, 384))
EARLY = [(0, 0)] + [(d, 0) for d in ORDER] + [(0, e) for e in ORDER] + [(d, 2) for d in ORDER] + [(2, 3), (2, 1), (3, 3), (3, 1)]
LATE = [(1, 3), (1, 1)]


def place():
    a, o = lax.axis_index("aux"), lax.axis_index("orb")
    return a // SIDE, a % SIDE, o // 2, o % 2


def tile_of(x, z, dx, dz):
    return (x + SIDE - dx) % SIDE * SIDE + (z + SIDE - dz) % SIDE


def fill(p, dx, dz, x, z, fin_ref, mask_ref, lhs, k):
    keep = mask_ref[pl.ds(tile_of(x, z, dx, dz), 1), :]
    rows = pl.ds(pl.multiple_of(k * BS, BS), BS)
    for j in range(NLB):
        block = fin_ref[p, dx, dz, j].astype(jnp.float32) * keep[:, j * BS : (j + 1) * BS]
        lhs[rows, j * BS : (j + 1) * BS] = block.astype(jnp.bfloat16)


def gram(half):
    return lax.dot_general(half, half, (((1,), (1,)), ((), ())), preferred_element_type=jnp.float32)


def gather_kernel(
    ints, panel, screen, owner, hv, fin, dens, mask, kacc,
    xa, zb, prcv, scr, own, lhs, s_one, r_one, s_two, r_fin, s_pan, r_pan, l_sem,
):
    x, z, y, c = place()
    o = y * 2 + c

    def at_xz(dx, dz):
        return ((x + dx) % SIDE * SIDE + (z + dz) % SIDE, o)

    def at_orb(dy, dc):
        return (x * SIDE + z, (y + dy) % SIDE * 2 + (c + dc) % 2)

    def send(src, dst, ss, rs, to):
        return pltpu.make_async_remote_copy(
            src_ref=src, dst_ref=dst, send_sem=ss, recv_sem=rs, device_id=to, device_id_type=MESH
        )

    barrier = pltpu.get_barrier_semaphore()
    for d in (1, 2, 3):
        for to in (at_xz(d, 0), at_xz(0, d), at_orb(d, 0)):
            pl.semaphore_signal(barrier, inc=1, device_id=to, device_id_type=MESH)
    pl.semaphore_signal(barrier, inc=1, device_id=at_orb(0, 1), device_id_type=MESH)
    pl.semaphore_wait(barrier, 10)

    relay_a, relay_b = {}, {}
    for d in ORDER:
        for e in ORDER:
            relay_a[d, e] = send(ints.at[0, (x + d) % SIDE, (z + e) % SIDE], xa.at[d - 1, e - 1], s_one.at[0, d, e], r_one.at[0, d, e], at_xz(d, 0))
            relay_b[d, e] = send(ints.at[1, (x + e) % SIDE, (z + d) % SIDE], zb.at[d - 1, e - 1], s_one.at[1, d, e], r_one.at[1, d, e], at_xz(0, d))
            relay_a[d, e].start()
            relay_b[d, e].start()
    panels = {d: send(panel.at[0], prcv.at[o], s_pan.at[0, d], r_pan.at[0, d], at_orb(d, 0)) for d in ORDER}
    for d in ORDER:
        panels[d].start()
    direct = []
    for d in ORDER:
        direct.append(send(ints.at[0, (x + d) % SIDE, z], fin.at[0, d, 0], s_one.at[0, d, 0], r_fin.at[0, d, 0], at_xz(d, 0)))
        direct.append(send(ints.at[1, x, (z + d) % SIDE], fin.at[1, 0, d], s_one.at[1, d, 0], r_fin.at[1, d, 0], at_xz(0, d)))
    for e in ORDER:
        direct.append(send(ints.at[0, x, (z + e) % SIDE], fin.at[0, 0, e], s_two.at[0, 0, e], r_fin.at[0, 0, e], at_xz(0, e)))
        direct.append(send(ints.at[1, (x + e) % SIDE, z], fin.at[1, e, 0], s_two.at[1, 0, e], r_fin.at[1, 0, e], at_xz(e, 0)))
    for copy in direct:
        copy.start()
    mine = [
        pltpu.make_async_copy(ints.at[0, x, z], fin.at[0, 0, 0], l_sem.at[0]),
        pltpu.make_async_copy(ints.at[1, x, z], fin.at[1, 0, 0], l_sem.at[1]),
        pltpu.make_async_copy(panel.at[0], prcv.at[o], l_sem.at[2]),
    ]
    row = o * SIDE * SIDE + x * SIDE + z
    masks = pltpu.make_async_copy(screen, scr, l_sem.at[3])
    masks.start()
    owners = pltpu.make_async_copy(owner, own, l_sem.at[4])
    owners.start()
    for copy in mine:
        copy.start()
    shared = {0: send(panel.at[0], prcv.at[o], s_pan.at[1, 0], r_pan.at[1, 0], at_orb(0, 1))}
    shared[0].start()

    masks.wait()
    pick = lax.broadcasted_iota(jnp.int32, (NAT, NLB, NRB), 2) == row
    kept = jnp.sum(jnp.where(pick, scr[...], 0).astype(jnp.float32), axis=2)
    wide = lax.broadcasted_iota(jnp.int32, (NLB, DEPTH), 1) // BS == lax.broadcasted_iota(jnp.int32, (NLB, DEPTH), 0)
    mask[...] = jnp.dot(kept, wide.astype(jnp.float32), preferred_element_type=jnp.float32)
    kacc[...] = jnp.zeros_like(kacc)

    for d in ORDER:
        panels[d].wait_recv()
        slot = (y + SIDE - d) % SIDE * 2 + c
        shared[d] = send(prcv.at[slot], prcv.at[slot], s_pan.at[1, d], r_pan.at[1, d], at_orb(0, 1))
        shared[d].start()

    second = {}
    for d in ORDER:
        for e in ORDER:
            second[0, d, e] = send(xa.at[d - 1, e - 1], fin.at[0, d, e], s_two.at[0, d, e], r_fin.at[0, d, e], at_xz(0, e))
            second[1, d, e] = send(zb.at[d - 1, e - 1], fin.at[1, e, d], s_two.at[1, d, e], r_fin.at[1, d, e], at_xz(e, 0))
    for d, e in EARLY[7:] + LATE:
        relay_a[d, e].wait_recv()
        second[0, d, e].start()
        relay_b[d, e].wait_recv()
        second[1, d, e].start()

    for d in range(SIDE):
        shared[d].wait_recv()
    mine[2].wait()
    owners.wait()
    for j in range(NLB):
        dens[j * BS : (j + 1) * BS, :] = prcv[own[j]]

    def pair(d, e):
        for p, (dx, dz) in ((0, (d, e)), (1, (e, d))):
            send(fin.at[p, dx, dz], fin.at[p, dx, dz], s_one.at[0, 0, 0], r_fin.at[p, d, e], at_xz(1, 0)).wait_recv()

    def work(d, e):
        spots = [tile_of(x, z, d, e) * 2, tile_of(x, z, e, d) * 2 + 1]
        fill(0, d, e, x, z, fin, mask, lhs, 0)
        fill(1, e, d, x, z, fin, mask, lhs, 1)
        for at, width in COLUMNS:
            product = jnp.dot(lhs[...], dens[:, at : at + width], preferred_element_type=jnp.float32)
            product = product.astype(jnp.bfloat16)
            for p in range(2):
                hv[pl.ds(spots[p], 1), :, at : at + width] = product[p * BS : (p + 1) * BS].reshape(1, BS, width)
        for p in range(2):
            kacc[...] += gram(hv[pl.ds(spots[p], 1)].reshape(BS, NOCC))

    mine[0].wait()
    mine[1].wait()
    work(0, 0)

    def step(g, _):
        d, e = pairs(g)
        pair(d, e)
        work(d, e)
        return 0

    lax.fori_loop(0, len(EARLY) - 1, step, 0)
    for d, e in LATE:
        pair(d, e)
    for copy in list(relay_a.values()) + list(relay_b.values()) + direct + list(second.values()) + list(panels.values()) + list(shared.values()):
        copy.wait_send()


def pairs(g):
    first, second, third = g // 3 == 0, g // 3 == 1, g // 3 == 2
    turn = (g + 1) % 3 + 1
    late = g - 9
    d = jnp.where(first | third, turn, jnp.where(second, 0, (late // 2 + 1) % 3 + 1))
    e = jnp.where(first, 0, jnp.where(second, turn, jnp.where(third, 2, 3 - late % 2 * 2)))
    return d, e


def finish_kernel(hv, fin, dens, mask, kacc, halves, kblocks, lhs, late, sems):
    x, z, y, c = place()
    copies = []

    def out(source, spot, count):
        copies.append(pltpu.make_async_copy(source, halves.at[0, pl.ds(spot, count)], sems.at[len(copies)]))
        copies[-1].start()

    left = [unit for d, e in LATE for unit in ((0, d, e), (1, e, d))]
    whole = [dx for dx in range(SIDE) if all(dx != unit[1] for unit in left)]
    for dx in whole:
        spot = (x + SIDE - dx) % SIDE * SIDE * 2
        out(hv.at[pl.ds(spot, 2 * SIDE)], spot, 2 * SIDE)
    rest = []
    for dx in range(SIDE):
        for dz in range(SIDE):
            ready = [p for p in range(2) if (p, dx, dz) not in left]
            if ready and dx not in whole:
                rest.append((tile_of(x, z, dx, dz) * 2 + ready[0], len(ready)))
    for spot, count in rest:
        out(hv.at[pl.ds(spot, count)], spot, count)

    def unit(k):
        d, e, p = 1, 3 - k // 2 * 2, k % 2
        return p, (1 - p) * d + p * e, (1 - p) * e + p * d

    def stage(k, _):
        p, dx, dz = unit(k)
        fill(p, dx, dz, x, z, fin, mask, lhs, k)
        return 0

    def column(i, _):
        at = pl.multiple_of(i * STEP, STEP)
        product = jnp.dot(lhs[...], dens[:, pl.ds(at, STEP)], preferred_element_type=jnp.float32)
        late[:, :, pl.ds(at, STEP)] = product.astype(jnp.bfloat16).reshape(len(left), BS, STEP)
        return 0

    lax.fori_loop(0, len(left), stage, 0)
    lax.fori_loop(0, NOCC // STEP, column, 0)
    for k in range(len(left)):
        p, dx, dz = unit(k)
        out(late.at[pl.ds(k, 1)], tile_of(x, z, dx, dz) * 2 + p, 1)
    total = lax.fori_loop(0, len(left), lambda k, total: total + gram(late[k]), kacc[...])
    kblocks[0] = total * SCALE
    for copy in copies:
        copy.wait()


def shards(integrals, panels, screen, owner_map):
    piece = (NLB, BS, BS)
    vmem = pl.BlockSpec(memory_space=pltpu.VMEM)
    hbm = pl.BlockSpec(memory_space=pl.ANY)
    dma = pltpu.SemaphoreType.DMA
    bf16, f32 = jnp.bfloat16, jnp.float32
    ints = integrals.reshape((2, SIDE, SIDE) + piece)
    between = pl.pallas_call(
        gather_kernel,
        name="gather",
        out_shape=[
            pltpu.VMEM((NAUX, BS, NOCC), bf16),
            pltpu.VMEM((2, SIDE, SIDE) + piece, bf16),
            pltpu.VMEM((DEPTH, NOCC), bf16),
            pltpu.VMEM((NAT, DEPTH), f32),
            pltpu.VMEM((BS, BS), f32),
        ],
        in_specs=[hbm] * 4,
        out_specs=[vmem] * 5,
        scratch_shapes=[
            pltpu.VMEM((3, 3) + piece, bf16),
            pltpu.VMEM((3, 3) + piece, bf16),
            pltpu.VMEM((NLB, BS, NOCC), bf16),
            pltpu.VMEM((NAT, NLB, NRB), jnp.int32),
            pltpu.SMEM((NLB,), jnp.int32),
            pltpu.VMEM((2 * BS, DEPTH), bf16),
            dma((2, 4, 4)),
            dma((2, 4, 4)),
            dma((2, 4, 4)),
            dma((2, 4, 4)),
            dma((2, 4)),
            dma((2, 4)),
            dma((5,)),
        ],
        compiler_params=pltpu.CompilerParams(collective_id=0, has_side_effects=True, vmem_limit_bytes=24 << 20),
        cost_estimate=pl.CostEstimate(flops=16 << 30, bytes_accessed=24 << 20, transcendentals=0),
    )(*(pltpu.with_memory_space_constraint(v, pltpu.HBM) for v in (ints, panels, screen.transpose(0, 2, 1), owner_map)))
    return pl.pallas_call(
        finish_kernel,
        name="finish",
        out_shape=[
            jax.ShapeDtypeStruct((1, NAUX, BS, NOCC), bf16),
            jax.ShapeDtypeStruct((1, BS, BS), f32),
        ],
        in_specs=[vmem] * 5,
        out_specs=[hbm, vmem],
        scratch_shapes=[
            pltpu.VMEM((2 * len(LATE) * BS, DEPTH), bf16),
            pltpu.VMEM((2 * len(LATE), BS, NOCC), bf16),
            dma((NAUX,)),
        ],
        compiler_params=pltpu.CompilerParams(vmem_limit_bytes=24 << 20),
        cost_estimate=pl.CostEstimate(flops=2 << 30, bytes_accessed=16 << 20, transcendentals=0),
    )(*(pltpu.with_memory_space_constraint(v, pltpu.VMEM) for v in between))


def solution(mesh):
    placed = (P("aux", "orb", None, None, None), P("orb", None, None), P(), P())
    return jax.shard_map(
        shards,
        mesh=mesh,
        in_specs=placed,
        out_specs=(P(("orb", "aux"), None, None, None), P(("orb", "aux"), None, None)),
        check_vma=False,
    )
```

```python
import functools

import jax
import jax.numpy as jnp
from jax import lax
from jax.experimental import pallas as pl
from jax.experimental.pallas import tpu as pltpu
from jax.sharding import PartitionSpec as P

MESH = pl.DeviceIdType.MESH
BS = 128
NLB = 8
NOCC = 1920
NAUX = 32
NAT = 16
NRB = 128
DEPTH = NLB * BS
SIDE = 4
SCALE = 1.0 / (NAUX * NOCC)
ORDER = (2, 3, 1)
STEP = 640
COLUMNS = ((0, 512), (512, 512), (1024, 512), (1536, 384))
PAIRS = [(d, 0) for d in (0,) + ORDER] + [(d, e) for d in (0,) + ORDER for e in ORDER]
EARLY, LATE = PAIRS[:14], PAIRS[14:]


def place():
    a, o = lax.axis_index("aux"), lax.axis_index("orb")
    return a // SIDE, a % SIDE, o // 2, o % 2


def tile_of(x, z, dx, dz):
    return (x + SIDE - dx) % SIDE * SIDE + (z + SIDE - dz) % SIDE


def fill(p, dx, dz, x, z, fin_ref, mask_ref, lhs, k):
    keep = mask_ref[pl.ds(tile_of(x, z, dx, dz), 1), :]
    rows = pl.ds(pl.multiple_of(k * BS, BS), BS)
    for j in range(NLB):
        block = fin_ref[p, dx, dz, j].astype(jnp.float32) * keep[:, j * BS : (j + 1) * BS]
        lhs[rows, j * BS : (j + 1) * BS] = block.astype(jnp.bfloat16)


def gram(half):
    return lax.dot_general(half, half, (((1,), (1,)), ((), ())), preferred_element_type=jnp.float32)


def gather_kernel(
    ints, panel, screen, owner, hv, fin, dens, mask, kacc,
    xa, zb, prcv, scr, own, lhs, s_one, r_one, s_two, r_fin, s_pan, r_pan, l_sem, d_sem,
):
    x, z, y, c = place()
    o = y * 2 + c

    def at_xz(dx, dz):
        return ((x + dx) % SIDE * SIDE + (z + dz) % SIDE, o)

    def at_orb(dy, dc):
        return (x * SIDE + z, (y + dy) % SIDE * 2 + (c + dc) % 2)

    def send(src, dst, ss, rs, to):
        return pltpu.make_async_remote_copy(
            src_ref=src, dst_ref=dst, send_sem=ss, recv_sem=rs, device_id=to, device_id_type=MESH
        )

    barrier = pltpu.get_barrier_semaphore()
    for d in (1, 2, 3):
        for to in (at_xz(d, 0), at_xz(0, d), at_orb(d, 0)):
            pl.semaphore_signal(barrier, inc=1, device_id=to, device_id_type=MESH)
    pl.semaphore_signal(barrier, inc=1, device_id=at_orb(0, 1), device_id_type=MESH)
    pl.semaphore_wait(barrier, 10)

    relay_a, relay_b = {}, {}
    for d in ORDER:
        relay_a[d] = send(ints.at[0, (x + d) % SIDE], xa.at[d - 1], s_one.at[0, d], r_one.at[0, d], at_xz(d, 0))
        relay_b[d] = send(ints.at[1, :, (z + d) % SIDE], zb.at[d - 1], s_one.at[1, d], r_one.at[1, d], at_xz(0, d))
        relay_a[d].start()
        relay_b[d].start()
    panels = {d: send(panel.at[0], prcv.at[o], s_pan.at[0, d], r_pan.at[0, d], at_orb(d, 0)) for d in ORDER}
    for d in ORDER:
        panels[d].start()
    direct = []
    for e in ORDER:
        direct.append(send(ints.at[0, x, (z + e) % SIDE], fin.at[0, 0, e], s_two.at[0, 0, e], r_fin.at[0, 0, e], at_xz(0, e)))
        direct.append(send(ints.at[1, (x + e) % SIDE, z], fin.at[1, e, 0], s_two.at[1, 0, e], r_fin.at[1, 0, e], at_xz(e, 0)))
    for copy in direct:
        copy.start()
    mine = [
        pltpu.make_async_copy(ints.at[0, x, z], fin.at[0, 0, 0], l_sem.at[0]),
        pltpu.make_async_copy(ints.at[1, x, z], fin.at[1, 0, 0], l_sem.at[1]),
        pltpu.make_async_copy(panel.at[0], prcv.at[o], l_sem.at[2]),
    ]
    row = o * SIDE * SIDE + x * SIDE + z
    masks = pltpu.make_async_copy(screen, scr, l_sem.at[3])
    masks.start()
    owners = pltpu.make_async_copy(owner, own, l_sem.at[4])
    owners.start()
    for copy in mine:
        copy.start()
    shared = {0: send(panel.at[0], prcv.at[o], s_pan.at[1, 0], r_pan.at[1, 0], at_orb(0, 1))}
    shared[0].start()

    masks.wait()
    pick = lax.broadcasted_iota(jnp.int32, (NAT, NLB, NRB), 2) == row
    kept = jnp.sum(jnp.where(pick, scr[...], 0).astype(jnp.float32), axis=2)
    wide = lax.broadcasted_iota(jnp.int32, (NLB, DEPTH), 1) // BS == lax.broadcasted_iota(jnp.int32, (NLB, DEPTH), 0)
    mask[...] = jnp.dot(kept, wide.astype(jnp.float32), preferred_element_type=jnp.float32)
    kacc[...] = jnp.zeros_like(kacc)

    for d in ORDER:
        panels[d].wait_recv()
        slot = (y + SIDE - d) % SIDE * 2 + c
        shared[d] = send(prcv.at[slot], prcv.at[slot], s_pan.at[1, d], r_pan.at[1, d], at_orb(0, 1))
        shared[d].start()

    second = {}
    for d in ORDER:
        relay_a[d].wait_recv()
        relay_b[d].wait_recv()
        for e in ORDER:
            second[0, d, e] = send(xa.at[d - 1, (z + e) % SIDE], fin.at[0, d, e], s_two.at[0, d, e], r_fin.at[0, d, e], at_xz(0, e))
            second[1, d, e] = send(zb.at[d - 1, (x + e) % SIDE], fin.at[1, e, d], s_two.at[1, d, e], r_fin.at[1, d, e], at_xz(e, 0))
            second[0, d, e].start()
            second[1, d, e].start()
        mine.append(pltpu.make_async_copy(xa.at[d - 1, z], fin.at[0, d, 0], d_sem.at[0, d]))
        mine.append(pltpu.make_async_copy(zb.at[d - 1, x], fin.at[1, 0, d], d_sem.at[1, d]))
        mine[-2].start()
        mine[-1].start()

    for d in range(SIDE):
        shared[d].wait_recv()
    for copy in mine:
        copy.wait()
    owners.wait()
    for j in range(NLB):
        dens[j * BS : (j + 1) * BS, :] = prcv[own[j]]

    def pair(d, e):
        for p, (dx, dz) in ((0, (d, e)), (1, (e, d))):
            send(fin.at[p, dx, dz], fin.at[p, dx, dz], s_one.at[0, 0], r_fin.at[p, d, e], at_xz(1, 0)).wait_recv()

    def work(d, e):
        spots = [tile_of(x, z, d, e) * 2, tile_of(x, z, e, d) * 2 + 1]
        fill(0, d, e, x, z, fin, mask, lhs, 0)
        fill(1, e, d, x, z, fin, mask, lhs, 1)
        for at, width in COLUMNS:
            product = jnp.dot(lhs[...], dens[:, at : at + width], preferred_element_type=jnp.float32)
            product = product.astype(jnp.bfloat16)
            for p in range(2):
                hv[pl.ds(spots[p], 1), :, at : at + width] = product[p * BS : (p + 1) * BS].reshape(1, BS, width)
        for p in range(2):
            kacc[...] += gram(hv[pl.ds(spots[p], 1)].reshape(BS, NOCC))

    def step(g, _):
        d, e = pair_at(g)

        @pl.when(g >= SIDE)
        def _():
            pair(d, e)

        work(d, e)
        return 0

    lax.fori_loop(0, len(EARLY), step, 0)
    for d, e in LATE:
        pair(d, e)
    for copy in list(relay_a.values()) + list(relay_b.values()) + direct + list(second.values()) + list(panels.values()) + list(shared.values()):
        copy.wait_send()


def pair_at(g):
    def turn(i):
        return (2 * i - i // 2) % SIDE

    h = lax.max(g - SIDE, 0)
    first = g < SIDE
    return jnp.where(first, turn(g), turn(h // 3)), jnp.where(first, 0, turn(h % 3 + 1))


def finish_kernel(hv, fin, dens, mask, kacc, halves, kblocks, lhs, late, kout, sems, k_sem):
    x, z, y, c = place()
    copies = []

    def out(source, spot, count):
        copies.append(pltpu.make_async_copy(source, halves.at[0, pl.ds(spot, count)], sems.at[len(copies)]))
        copies[-1].start()

    left = [unit for d, e in LATE for unit in ((0, d, e), (1, e, d))]
    whole = [dx for dx in range(SIDE) if all(dx != unit[1] for unit in left)]
    for dx in whole:
        spot = (x + SIDE - dx) % SIDE * SIDE * 2
        out(hv.at[pl.ds(spot, 2 * SIDE)], spot, 2 * SIDE)
    rest = []
    for dx in range(SIDE):
        for dz in range(SIDE):
            ready = [p for p in range(2) if (p, dx, dz) not in left]
            if ready and dx not in whole:
                rest.append((tile_of(x, z, dx, dz) * 2 + ready[0], len(ready)))
    for spot, count in rest:
        out(hv.at[pl.ds(spot, count)], spot, count)

    def unit(k):
        d, e, p = 1, 3 - k // 2 * 2, k % 2
        return p, (1 - p) * d + p * e, (1 - p) * e + p * d

    def stage(k, _):
        p, dx, dz = unit(k)
        fill(p, dx, dz, x, z, fin, mask, lhs, k)
        return 0

    def column(i, _):
        at = pl.multiple_of(i * STEP, STEP)
        product = jnp.dot(lhs[...], dens[:, pl.ds(at, STEP)], preferred_element_type=jnp.float32)
        late[:, :, pl.ds(at, STEP)] = product.astype(jnp.bfloat16).reshape(len(left), BS, STEP)
        return 0

    lax.fori_loop(0, len(left), stage, 0)
    lax.fori_loop(0, NOCC // STEP, column, 0)
    for k in range(len(left)):
        p, dx, dz = unit(k)
        out(late.at[pl.ds(k, 1)], tile_of(x, z, dx, dz) * 2 + p, 1)
    total = lax.fori_loop(0, len(left), lambda k, total: total + gram(late[k]), kacc[...])
    kout[0] = total * SCALE
    copies.append(pltpu.make_async_copy(kout, kblocks, k_sem))
    copies[-1].start()
    for copy in copies:
        copy.wait()


def shards(integrals, panels, screen, owner_map):
    piece = (NLB, BS, BS)
    vmem = pl.BlockSpec(memory_space=pltpu.VMEM)
    hbm = pl.BlockSpec(memory_space=pl.ANY)
    dma = pltpu.SemaphoreType.DMA
    bf16, f32 = jnp.bfloat16, jnp.float32
    ints = integrals.reshape((2, SIDE, SIDE) + piece)
    between = pl.pallas_call(
        gather_kernel,
        name="gather",
        out_shape=[
            pltpu.VMEM((NAUX, BS, NOCC), bf16),
            pltpu.VMEM((2, SIDE, SIDE) + piece, bf16),
            pltpu.VMEM((DEPTH, NOCC), bf16),
            pltpu.VMEM((NAT, DEPTH), f32),
            pltpu.VMEM((BS, BS), f32),
        ],
        in_specs=[hbm] * 4,
        out_specs=[vmem] * 5,
        scratch_shapes=[
            pltpu.VMEM((3, SIDE) + piece, bf16),
            pltpu.VMEM((3, SIDE) + piece, bf16),
            pltpu.VMEM((NLB, BS, NOCC), bf16),
            pltpu.VMEM((NAT, NLB, NRB), jnp.int32),
            pltpu.SMEM((NLB,), jnp.int32),
            pltpu.VMEM((2 * BS, DEPTH), bf16),
            dma((2, 4)),
            dma((2, 4)),
            dma((2, 4, 4)),
            dma((2, 4, 4)),
            dma((2, 4)),
            dma((2, 4)),
            dma((5,)),
            dma((2, 4)),
        ],
        compiler_params=pltpu.CompilerParams(collective_id=0, has_side_effects=True, vmem_limit_bytes=24 << 20),
        cost_estimate=pl.CostEstimate(flops=16 << 30, bytes_accessed=24 << 20, transcendentals=0),
    )(*(pltpu.with_memory_space_constraint(v, pltpu.HBM) for v in (ints, panels, screen.transpose(0, 2, 1), owner_map)))
    return pl.pallas_call(
        finish_kernel,
        name="finish",
        out_shape=[
            pltpu.HBM((1, NAUX, BS, NOCC), bf16),
            pltpu.HBM((1, BS, BS), f32),
        ],
        in_specs=[vmem] * 5,
        out_specs=[hbm, hbm],
        scratch_shapes=[
            pltpu.VMEM((2 * len(LATE) * BS, DEPTH), bf16),
            pltpu.VMEM((2 * len(LATE), BS, NOCC), bf16),
            pltpu.VMEM((1, BS, BS), f32),
            dma((NAUX,)),
            dma(()),
        ],
        compiler_params=pltpu.CompilerParams(vmem_limit_bytes=24 << 20),
        cost_estimate=pl.CostEstimate(flops=2 << 30, bytes_accessed=16 << 20, transcendentals=0),
    )(*(pltpu.with_memory_space_constraint(v, pltpu.VMEM) for v in between))


def solution(mesh):
    placed = (P("aux", "orb", None, None, None), P("orb", None, None), P(), P())
    return jax.shard_map(
        shards,
        mesh=mesh,
        in_specs=placed,
        out_specs=(P(("orb", "aux"), None, None, None), P(("orb", "aux"), None, None)),
        check_vma=False,
    )
```

```python
import functools

import jax
import jax.numpy as jnp
from jax import lax
from jax.experimental import pallas as pl
from jax.experimental.pallas import tpu as pltpu
from jax.sharding import PartitionSpec as P

MESH = pl.DeviceIdType.MESH
BS = 128
NLB = 8
NOCC = 1920
NAUX = 32
NAT = 16
NRB = 128
DEPTH = NLB * BS
SIDE = 4
SCALE = 1.0 / (NAUX * NOCC)
SENDS = (1, 3, 2)
ORDER = (2, 3, 1)
TURNS = (2, 3, 1)
STEP = 640
COLUMNS = ((0, 512), (512, 512), (1024, 512), (1536, 384))
PAIRS = [(d, 0) for d in (0,) + ORDER] + [(d, e) for d in (0,) + ORDER for e in TURNS]
EARLY, LATE = PAIRS[:14], PAIRS[14:]


def place():
    a, o = lax.axis_index("aux"), lax.axis_index("orb")
    return a // SIDE, a % SIDE, o // 2, o % 2


def tile_of(x, z, dx, dz):
    return (x + SIDE - dx) % SIDE * SIDE + (z + SIDE - dz) % SIDE


def fill(p, dx, dz, x, z, fin_ref, mask_ref, lhs, k):
    keep = mask_ref[pl.ds(tile_of(x, z, dx, dz), 1), :]
    rows = pl.ds(pl.multiple_of(k * BS, BS), BS)
    for j in range(NLB):
        block = fin_ref[p, dx, dz, j].astype(jnp.float32) * keep[:, j * BS : (j + 1) * BS]
        lhs[rows, j * BS : (j + 1) * BS] = block.astype(jnp.bfloat16)


def gram(half):
    return lax.dot_general(half, half, (((1,), (1,)), ((), ())), preferred_element_type=jnp.float32)


def gather_kernel(
    ints, panel, screen, owner, hv, fin, dens, mask, kacc,
    xa, zb, prcv, scr, own, lhs, s_one, r_one, s_two, r_fin, s_pan, r_pan, l_sem, d_sem,
):
    x, z, y, c = place()
    o = y * 2 + c

    def at_xz(dx, dz):
        return ((x + dx) % SIDE * SIDE + (z + dz) % SIDE, o)

    def at_orb(dy, dc):
        return (x * SIDE + z, (y + dy) % SIDE * 2 + (c + dc) % 2)

    def send(src, dst, ss, rs, to):
        return pltpu.make_async_remote_copy(
            src_ref=src, dst_ref=dst, send_sem=ss, recv_sem=rs, device_id=to, device_id_type=MESH
        )

    barrier = pltpu.get_barrier_semaphore()
    for d in (1, 2, 3):
        for to in (at_xz(d, 0), at_xz(0, d), at_orb(d, 0)):
            pl.semaphore_signal(barrier, inc=1, device_id=to, device_id_type=MESH)
    pl.semaphore_signal(barrier, inc=1, device_id=at_orb(0, 1), device_id_type=MESH)
    pl.semaphore_wait(barrier, 10)

    relay_a, relay_b = {}, {}
    for d in SENDS:
        relay_a[d] = send(ints.at[0, (x + d) % SIDE], xa.at[d - 1], s_one.at[0, d], r_one.at[0, d], at_xz(d, 0))
        relay_b[d] = send(ints.at[1, :, (z + d) % SIDE], zb.at[d - 1], s_one.at[1, d], r_one.at[1, d], at_xz(0, d))
        relay_a[d].start()
        relay_b[d].start()
    panels = {d: send(panel.at[0], prcv.at[o], s_pan.at[0, d], r_pan.at[0, d], at_orb(d, 0)) for d in ORDER}
    for d in ORDER:
        panels[d].start()
    direct = []
    for e in TURNS:
        direct.append(send(ints.at[0, x, (z + e) % SIDE], fin.at[0, 0, e], s_two.at[0, 0, e], r_fin.at[0, 0, e], at_xz(0, e)))
        direct.append(send(ints.at[1, (x + e) % SIDE, z], fin.at[1, e, 0], s_two.at[1, 0, e], r_fin.at[1, 0, e], at_xz(e, 0)))
    for copy in direct:
        copy.start()
    mine = [
        pltpu.make_async_copy(ints.at[0, x, z], fin.at[0, 0, 0], l_sem.at[0]),
        pltpu.make_async_copy(ints.at[1, x, z], fin.at[1, 0, 0], l_sem.at[1]),
        pltpu.make_async_copy(panel.at[0], prcv.at[o], l_sem.at[2]),
    ]
    row = o * SIDE * SIDE + x * SIDE + z
    masks = pltpu.make_async_copy(screen, scr, l_sem.at[3])
    masks.start()
    owners = pltpu.make_async_copy(owner, own, l_sem.at[4])
    owners.start()
    for copy in mine:
        copy.start()
    shared = {0: send(panel.at[0], prcv.at[o], s_pan.at[1, 0], r_pan.at[1, 0], at_orb(0, 1))}
    shared[0].start()

    masks.wait()
    pick = lax.broadcasted_iota(jnp.int32, (NAT, NLB, NRB), 2) == row
    kept = jnp.sum(jnp.where(pick, scr[...], 0).astype(jnp.float32), axis=2)
    wide = lax.broadcasted_iota(jnp.int32, (NLB, DEPTH), 1) // BS == lax.broadcasted_iota(jnp.int32, (NLB, DEPTH), 0)
    mask[...] = jnp.dot(kept, wide.astype(jnp.float32), preferred_element_type=jnp.float32)
    kacc[...] = jnp.zeros_like(kacc)

    for d in ORDER:
        panels[d].wait_recv()
        slot = (y + SIDE - d) % SIDE * 2 + c
        shared[d] = send(prcv.at[slot], prcv.at[slot], s_pan.at[1, d], r_pan.at[1, d], at_orb(0, 1))
        shared[d].start()

    second = {}
    for d in ORDER:
        relay_a[d].wait_recv()
        relay_b[d].wait_recv()
        for e in TURNS:
            second[0, d, e] = send(xa.at[d - 1, (z + e) % SIDE], fin.at[0, d, e], s_two.at[0, d, e], r_fin.at[0, d, e], at_xz(0, e))
            second[1, d, e] = send(zb.at[d - 1, (x + e) % SIDE], fin.at[1, e, d], s_two.at[1, d, e], r_fin.at[1, d, e], at_xz(e, 0))
            second[0, d, e].start()
            second[1, d, e].start()
        mine.append(pltpu.make_async_copy(xa.at[d - 1, z], fin.at[0, d, 0], d_sem.at[0, d]))
        mine.append(pltpu.make_async_copy(zb.at[d - 1, x], fin.at[1, 0, d], d_sem.at[1, d]))
        mine[-2].start()
        mine[-1].start()

    for d in range(SIDE):
        shared[d].wait_recv()
    for copy in mine:
        copy.wait()
    owners.wait()
    for j in range(NLB):
        dens[j * BS : (j + 1) * BS, :] = prcv[own[j]]

    def pair(d, e):
        for p, (dx, dz) in ((0, (d, e)), (1, (e, d))):
            send(fin.at[p, dx, dz], fin.at[p, dx, dz], s_one.at[0, 0], r_fin.at[p, d, e], at_xz(1, 0)).wait_recv()

    def work(d, e):
        spots = [tile_of(x, z, d, e) * 2, tile_of(x, z, e, d) * 2 + 1]
        fill(0, d, e, x, z, fin, mask, lhs, 0)
        fill(1, e, d, x, z, fin, mask, lhs, 1)
        for at, width in COLUMNS:
            product = jnp.dot(lhs[...], dens[:, at : at + width], preferred_element_type=jnp.float32)
            product = product.astype(jnp.bfloat16)
            for p in range(2):
                hv[pl.ds(spots[p], 1), :, at : at + width] = product[p * BS : (p + 1) * BS].reshape(1, BS, width)
        for p in range(2):
            kacc[...] += gram(hv[pl.ds(spots[p], 1)].reshape(BS, NOCC))

    def step(g, _):
        d, e = pair_at(g)

        @pl.when(g >= SIDE)
        def _():
            pair(d, e)

        work(d, e)
        return 0

    lax.fori_loop(0, len(EARLY), step, 0)
    for copy in list(relay_a.values()) + list(relay_b.values()) + direct + list(second.values()) + list(panels.values()) + list(shared.values()):
        copy.wait_send()
    for d, e in LATE:
        pair(d, e)


def pair_at(g):
    h = lax.max(g - SIDE, 0)
    first = g < SIDE
    return pick(jnp.where(first, g, h // 3), (0,) + ORDER), jnp.where(first, 0, pick(h % 3, TURNS))


def pick(i, values):
    result = values[-1]
    for k in range(len(values) - 2, -1, -1):
        result = jnp.where(i == k, values[k], result)
    return result


def finish_kernel(hv, fin, dens, mask, kacc, halves, kblocks, lhs, late, kout, sems, k_sem):
    x, z, y, c = place()
    copies = []

    def out(source, spot, count):
        copies.append(pltpu.make_async_copy(source, halves.at[0, pl.ds(spot, count)], sems.at[len(copies)]))
        copies[-1].start()

    left = [unit for d, e in LATE for unit in ((0, d, e), (1, e, d))]
    whole = [dx for dx in range(SIDE) if all(dx != unit[1] for unit in left)]
    for dx in whole:
        spot = (x + SIDE - dx) % SIDE * SIDE * 2
        out(hv.at[pl.ds(spot, 2 * SIDE)], spot, 2 * SIDE)
    rest = []
    for dx in range(SIDE):
        for dz in range(SIDE):
            ready = [p for p in range(2) if (p, dx, dz) not in left]
            if ready and dx not in whole:
                rest.append((tile_of(x, z, dx, dz) * 2 + ready[0], len(ready)))
    for spot, count in rest:
        out(hv.at[pl.ds(spot, count)], spot, count)

    def unit(k):
        d, e, p = pick(k // 2, [pair[0] for pair in LATE]), pick(k // 2, [pair[1] for pair in LATE]), k % 2
        return p, (1 - p) * d + p * e, (1 - p) * e + p * d

    def stage(k, _):
        p, dx, dz = unit(k)
        fill(p, dx, dz, x, z, fin, mask, lhs, k)
        return 0

    def column(i, _):
        at = pl.multiple_of(i * STEP, STEP)
        product = jnp.dot(lhs[...], dens[:, pl.ds(at, STEP)], preferred_element_type=jnp.float32)
        late[:, :, pl.ds(at, STEP)] = product.astype(jnp.bfloat16).reshape(len(left), BS, STEP)
        return 0

    lax.fori_loop(0, len(left), stage, 0)
    lax.fori_loop(0, NOCC // STEP, column, 0)
    for k in range(len(left)):
        p, dx, dz = unit(k)
        out(late.at[pl.ds(k, 1)], tile_of(x, z, dx, dz) * 2 + p, 1)
    total = lax.fori_loop(0, len(left), lambda k, total: total + gram(late[k]), kacc[...])
    kout[0] = total * SCALE
    copies.append(pltpu.make_async_copy(kout, kblocks, k_sem))
    copies[-1].start()
    for copy in copies:
        copy.wait()


def shards(integrals, panels, screen, owner_map):
    piece = (NLB, BS, BS)
    vmem = pl.BlockSpec(memory_space=pltpu.VMEM)
    hbm = pl.BlockSpec(memory_space=pl.ANY)
    dma = pltpu.SemaphoreType.DMA
    bf16, f32 = jnp.bfloat16, jnp.float32
    ints = integrals.reshape((2, SIDE, SIDE) + piece)
    between = pl.pallas_call(
        gather_kernel,
        name="gather",
        out_shape=[
            pltpu.VMEM((NAUX, BS, NOCC), bf16),
            pltpu.VMEM((2, SIDE, SIDE) + piece, bf16),
            pltpu.VMEM((DEPTH, NOCC), bf16),
            pltpu.VMEM((NAT, DEPTH), f32),
            pltpu.VMEM((BS, BS), f32),
        ],
        in_specs=[hbm] * 4,
        out_specs=[vmem] * 5,
        scratch_shapes=[
            pltpu.VMEM((3, SIDE) + piece, bf16),
            pltpu.VMEM((3, SIDE) + piece, bf16),
            pltpu.VMEM((NLB, BS, NOCC), bf16),
            pltpu.VMEM((NAT, NLB, NRB), jnp.int32),
            pltpu.SMEM((NLB,), jnp.int32),
            pltpu.VMEM((2 * BS, DEPTH), bf16),
            dma((2, 4)),
            dma((2, 4)),
            dma((2, 4, 4)),
            dma((2, 4, 4)),
            dma((2, 4)),
            dma((2, 4)),
            dma((5,)),
            dma((2, 4)),
        ],
        compiler_params=pltpu.CompilerParams(collective_id=0, has_side_effects=True, vmem_limit_bytes=24 << 20),
        cost_estimate=pl.CostEstimate(flops=16 << 30, bytes_accessed=24 << 20, transcendentals=0),
    )(*(pltpu.with_memory_space_constraint(v, pltpu.HBM) for v in (ints, panels, screen.transpose(0, 2, 1), owner_map)))
    return pl.pallas_call(
        finish_kernel,
        name="finish",
        out_shape=[
            pltpu.HBM((1, NAUX, BS, NOCC), bf16),
            pltpu.HBM((1, BS, BS), f32),
        ],
        in_specs=[vmem] * 5,
        out_specs=[hbm, hbm],
        scratch_shapes=[
            pltpu.VMEM((2 * len(LATE) * BS, DEPTH), bf16),
            pltpu.VMEM((2 * len(LATE), BS, NOCC), bf16),
            pltpu.VMEM((1, BS, BS), f32),
            dma((NAUX,)),
            dma(()),
        ],
        compiler_params=pltpu.CompilerParams(vmem_limit_bytes=24 << 20),
        cost_estimate=pl.CostEstimate(flops=2 << 30, bytes_accessed=16 << 20, transcendentals=0),
    )(*(pltpu.with_memory_space_constraint(v, pltpu.VMEM) for v in between))


def solution(mesh):
    placed = (P("aux", "orb", None, None, None), P("orb", None, None), P(), P())
    return jax.shard_map(
        shards,
        mesh=mesh,
        in_specs=placed,
        out_specs=(P(("orb", "aux"), None, None, None), P(("orb", "aux"), None, None)),
        check_vma=False,
    )
```

```python
import functools

import jax
import jax.numpy as jnp
from jax import lax
from jax.experimental import pallas as pl
from jax.experimental.pallas import tpu as pltpu
from jax.sharding import PartitionSpec as P

MESH = pl.DeviceIdType.MESH
BS = 128
NLB = 8
NOCC = 1920
NAUX = 32
NAT = 16
NRB = 128
DEPTH = NLB * BS
SIDE = 4
SCALE = 1.0 / (NAUX * NOCC)
SENDS = (1, 3, 2)
ORDER = (2, 3, 1)
TURNS = (2, 3, 1)
STEP = 640
COLUMNS = ((0, 512), (512, 512), (1024, 512), (1536, 384))
PAIRS = [(d, 0) for d in (0,) + ORDER] + [(d, e) for d in (0,) + ORDER for e in TURNS]
EARLY, LATE = PAIRS[:14], PAIRS[14:]


def place():
    a, o = lax.axis_index("aux"), lax.axis_index("orb")
    return a // SIDE, a % SIDE, o // 2, o % 2


def tile_of(x, z, dx, dz):
    return (x + SIDE - dx) % SIDE * SIDE + (z + SIDE - dz) % SIDE


def fill(p, dx, dz, x, z, fin_ref, mask_ref, lhs, k):
    keep = mask_ref[pl.ds(tile_of(x, z, dx, dz), 1), :]
    rows = pl.ds(pl.multiple_of(k * BS, BS), BS)
    for j in range(NLB):
        block = fin_ref[p, dx, dz, j].astype(jnp.float32) * keep[:, j * BS : (j + 1) * BS]
        lhs[rows, j * BS : (j + 1) * BS] = block.astype(jnp.bfloat16)


def gram(half):
    return lax.dot_general(half, half, (((1,), (1,)), ((), ())), preferred_element_type=jnp.float32)


def gather_kernel(
    ints, panel, screen, owner, hv, fin, dens, mask, kacc,
    xa, zb, prcv, scr, own, lhs, s_one, r_one, s_two, r_fin, s_pan, r_pan, l_sem, d_sem,
):
    x, z, y, c = place()
    o = y * 2 + c

    def at_xz(dx, dz):
        return ((x + dx) % SIDE * SIDE + (z + dz) % SIDE, o)

    def at_orb(dy, dc):
        return (x * SIDE + z, (y + dy) % SIDE * 2 + (c + dc) % 2)

    def send(src, dst, ss, rs, to):
        return pltpu.make_async_remote_copy(
            src_ref=src, dst_ref=dst, send_sem=ss, recv_sem=rs, device_id=to, device_id_type=MESH
        )

    barrier = pltpu.get_barrier_semaphore()
    for d in (1, 2, 3):
        for to in (at_xz(d, 0), at_xz(0, d), at_orb(d, 0)):
            pl.semaphore_signal(barrier, inc=1, device_id=to, device_id_type=MESH)
    pl.semaphore_signal(barrier, inc=1, device_id=at_orb(0, 1), device_id_type=MESH)
    pl.semaphore_wait(barrier, 10)

    relay_a, relay_b = {}, {}
    for d in SENDS:
        relay_a[d] = send(ints.at[0, (x + d) % SIDE], xa.at[d - 1], s_one.at[0], r_one.at[0, d - 1], at_xz(d, 0))
        relay_b[d] = send(ints.at[1, :, (z + d) % SIDE], zb.at[d - 1], s_one.at[1], r_one.at[1, d - 1], at_xz(0, d))
        relay_a[d].start()
        relay_b[d].start()
    panels = {d: send(panel.at[0], prcv.at[o], s_pan.at[0], r_pan.at[0, d], at_orb(d, 0)) for d in ORDER}
    for d in ORDER:
        panels[d].start()
    direct = []
    for e in TURNS:
        direct.append(send(ints.at[0, x, (z + e) % SIDE], fin.at[0, 0, e], s_two.at[0], r_fin.at[0, 0, e - 1], at_xz(0, e)))
        direct.append(send(ints.at[1, (x + e) % SIDE, z], fin.at[1, e, 0], s_two.at[1], r_fin.at[1, 0, e - 1], at_xz(e, 0)))
    for copy in direct:
        copy.start()
    mine = [
        pltpu.make_async_copy(ints.at[0, x, z], fin.at[0, 0, 0], l_sem.at[0]),
        pltpu.make_async_copy(ints.at[1, x, z], fin.at[1, 0, 0], l_sem.at[1]),
        pltpu.make_async_copy(panel.at[0], prcv.at[o], l_sem.at[2]),
    ]
    row = o * SIDE * SIDE + x * SIDE + z
    masks = pltpu.make_async_copy(screen, scr, l_sem.at[3])
    masks.start()
    owners = pltpu.make_async_copy(owner, own, l_sem.at[4])
    owners.start()
    for copy in mine:
        copy.start()
    shared = {0: send(panel.at[0], prcv.at[o], s_pan.at[1], r_pan.at[1, 0], at_orb(0, 1))}
    shared[0].start()

    masks.wait()
    pick = lax.broadcasted_iota(jnp.int32, (NAT, NLB, NRB), 2) == row
    kept = jnp.sum(jnp.where(pick, scr[...], 0).astype(jnp.float32), axis=2)
    wide = lax.broadcasted_iota(jnp.int32, (NLB, DEPTH), 1) // BS == lax.broadcasted_iota(jnp.int32, (NLB, DEPTH), 0)
    mask[...] = jnp.dot(kept, wide.astype(jnp.float32), preferred_element_type=jnp.float32)
    kacc[...] = jnp.zeros_like(kacc)

    for d in ORDER:
        panels[d].wait_recv()
        slot = (y + SIDE - d) % SIDE * 2 + c
        shared[d] = send(prcv.at[slot], prcv.at[slot], s_pan.at[1], r_pan.at[1, d], at_orb(0, 1))
        shared[d].start()

    second = {}
    for d in ORDER:
        relay_a[d].wait_recv()
        relay_b[d].wait_recv()
        for e in TURNS:
            second[0, d, e] = send(xa.at[d - 1, (z + e) % SIDE], fin.at[0, d, e], s_two.at[0], r_fin.at[0, d, e - 1], at_xz(0, e))
            second[1, d, e] = send(zb.at[d - 1, (x + e) % SIDE], fin.at[1, e, d], s_two.at[1], r_fin.at[1, d, e - 1], at_xz(e, 0))
            second[0, d, e].start()
            second[1, d, e].start()
        mine.append(pltpu.make_async_copy(xa.at[d - 1, z], fin.at[0, d, 0], d_sem.at[0, d - 1]))
        mine.append(pltpu.make_async_copy(zb.at[d - 1, x], fin.at[1, 0, d], d_sem.at[1, d - 1]))
        mine[-2].start()
        mine[-1].start()

    for d in range(SIDE):
        shared[d].wait_recv()
    for copy in mine:
        copy.wait()
    owners.wait()
    for j in range(NLB):
        dens[j * BS : (j + 1) * BS, :] = prcv[own[j]]

    def pair(d, e):
        for p, (dx, dz) in ((0, (d, e)), (1, (e, d))):
            send(fin.at[p, dx, dz], fin.at[p, dx, dz], s_one.at[0], r_fin.at[p, d, e - 1], at_xz(1, 0)).wait_recv()

    def work(d, e):
        spots = [tile_of(x, z, d, e) * 2, tile_of(x, z, e, d) * 2 + 1]
        fill(0, d, e, x, z, fin, mask, lhs, 0)
        fill(1, e, d, x, z, fin, mask, lhs, 1)
        for at, width in COLUMNS:
            product = jnp.dot(lhs[...], dens[:, at : at + width], preferred_element_type=jnp.float32)
            product = product.astype(jnp.bfloat16)
            for p in range(2):
                hv[pl.ds(spots[p], 1), :, at : at + width] = product[p * BS : (p + 1) * BS].reshape(1, BS, width)
        for p in range(2):
            kacc[...] += gram(hv[pl.ds(spots[p], 1)].reshape(BS, NOCC))

    def step(g, _):
        d, e = pair_at(g)

        @pl.when(g >= SIDE)
        def _():
            pair(d, e)

        work(d, e)
        return 0

    lax.fori_loop(0, len(EARLY), step, 0)
    for whole, sem in (
        (xa, s_one.at[0]), (zb, s_one.at[1]), (xa, s_two.at[0]), (zb, s_two.at[1]),
        (prcv.at[pl.ds(0, 3)], s_pan.at[0]), (prcv.at[pl.ds(0, 4)], s_pan.at[1]),
    ):
        send(whole, whole, sem, r_fin.at[0, 0, 0], at_xz(1, 0)).wait_send()
    for d, e in LATE:
        pair(d, e)


def pair_at(g):
    h = lax.max(g - SIDE, 0)
    first = g < SIDE
    return pick(jnp.where(first, g, h // 3), (0,) + ORDER), jnp.where(first, 0, pick(h % 3, TURNS))


def pick(i, values):
    result = values[-1]
    for k in range(len(values) - 2, -1, -1):
        result = jnp.where(i == k, values[k], result)
    return result


def finish_kernel(hv, fin, dens, mask, kacc, halves, kblocks, lhs, late, kout, sem, k_sem):
    x, z, y, c = place()
    def out(source, spot, count):
        pltpu.make_async_copy(source, halves.at[0, pl.ds(spot, count)], sem).start()

    left = [unit for d, e in LATE for unit in ((0, d, e), (1, e, d))]
    whole = [dx for dx in range(SIDE) if all(dx != unit[1] for unit in left)]
    for dx in whole:
        spot = (x + SIDE - dx) % SIDE * SIDE * 2
        out(hv.at[pl.ds(spot, 2 * SIDE)], spot, 2 * SIDE)
    rest = []
    for dx in range(SIDE):
        for dz in range(SIDE):
            ready = [p for p in range(2) if (p, dx, dz) not in left]
            if ready and dx not in whole:
                rest.append((tile_of(x, z, dx, dz) * 2 + ready[0], len(ready)))
    for spot, count in rest:
        out(hv.at[pl.ds(spot, count)], spot, count)

    def unit(k):
        d, e, p = pick(k // 2, [pair[0] for pair in LATE]), pick(k // 2, [pair[1] for pair in LATE]), k % 2
        return p, (1 - p) * d + p * e, (1 - p) * e + p * d

    def stage(k, _):
        p, dx, dz = unit(k)
        fill(p, dx, dz, x, z, fin, mask, lhs, k)
        return 0

    def column(i, _):
        at = pl.multiple_of(i * STEP, STEP)
        product = jnp.dot(lhs[...], dens[:, pl.ds(at, STEP)], preferred_element_type=jnp.float32)
        late[:, :, pl.ds(at, STEP)] = product.astype(jnp.bfloat16).reshape(len(left), BS, STEP)
        return 0

    lax.fori_loop(0, len(left), stage, 0)
    lax.fori_loop(0, NOCC // STEP, column, 0)
    for k in range(len(left)):
        p, dx, dz = unit(k)
        out(late.at[pl.ds(k, 1)], tile_of(x, z, dx, dz) * 2 + p, 1)
    total = lax.fori_loop(0, len(left), lambda k, total: total + gram(late[k]), kacc[...])
    kout[0] = total * SCALE
    last = pltpu.make_async_copy(kout, kblocks, k_sem)
    last.start()
    pltpu.make_async_copy(hv, halves.at[0], sem).wait()
    last.wait()


def shards(integrals, panels, screen, owner_map):
    piece = (NLB, BS, BS)
    vmem = pl.BlockSpec(memory_space=pltpu.VMEM)
    hbm = pl.BlockSpec(memory_space=pl.ANY)
    dma = pltpu.SemaphoreType.DMA
    bf16, f32 = jnp.bfloat16, jnp.float32
    ints = integrals.reshape((2, SIDE, SIDE) + piece)
    between = pl.pallas_call(
        gather_kernel,
        name="gather",
        out_shape=[
            pltpu.VMEM((NAUX, BS, NOCC), bf16),
            pltpu.VMEM((2, SIDE, SIDE) + piece, bf16),
            pltpu.VMEM((DEPTH, NOCC), bf16),
            pltpu.VMEM((NAT, DEPTH), f32),
            pltpu.VMEM((BS, BS), f32),
        ],
        in_specs=[hbm] * 4,
        out_specs=[vmem] * 5,
        scratch_shapes=[
            pltpu.VMEM((3, SIDE) + piece, bf16),
            pltpu.VMEM((3, SIDE) + piece, bf16),
            pltpu.VMEM((NLB, BS, NOCC), bf16),
            pltpu.VMEM((NAT, NLB, NRB), jnp.int32),
            pltpu.SMEM((NLB,), jnp.int32),
            pltpu.VMEM((2 * BS, DEPTH), bf16),
            dma((2,)),
            dma((2, 3)),
            dma((2,)),
            dma((2, 4, 3)),
            dma((2,)),
            dma((2, 4)),
            dma((5,)),
            dma((2, 3)),
        ],
        compiler_params=pltpu.CompilerParams(collective_id=0, has_side_effects=True, vmem_limit_bytes=24 << 20),
        cost_estimate=pl.CostEstimate(flops=16 << 30, bytes_accessed=24 << 20, transcendentals=0),
    )(*(pltpu.with_memory_space_constraint(v, pltpu.HBM) for v in (ints, panels, screen.transpose(0, 2, 1), owner_map)))
    return pl.pallas_call(
        finish_kernel,
        name="finish",
        out_shape=[
            pltpu.HBM((1, NAUX, BS, NOCC), bf16),
            pltpu.HBM((1, BS, BS), f32),
        ],
        in_specs=[vmem] * 5,
        out_specs=[hbm, hbm],
        scratch_shapes=[
            pltpu.VMEM((2 * len(LATE) * BS, DEPTH), bf16),
            pltpu.VMEM((2 * len(LATE), BS, NOCC), bf16),
            pltpu.VMEM((1, BS, BS), f32),
            dma(()),
            dma(()),
        ],
        compiler_params=pltpu.CompilerParams(vmem_limit_bytes=24 << 20),
        cost_estimate=pl.CostEstimate(flops=2 << 30, bytes_accessed=16 << 20, transcendentals=0),
    )(*(pltpu.with_memory_space_constraint(v, pltpu.VMEM) for v in between))


def solution(mesh):
    placed = (P("aux", "orb", None, None, None), P("orb", None, None), P(), P())
    return jax.shard_map(
        shards,
        mesh=mesh,
        in_specs=placed,
        out_specs=(P(("orb", "aux"), None, None, None), P(("orb", "aux"), None, None)),
        check_vma=False,
    )
```

```python
import functools

import jax
import jax.numpy as jnp
from jax import lax
from jax.experimental import pallas as pl
from jax.experimental.pallas import tpu as pltpu
from jax.sharding import PartitionSpec as P

MESH = pl.DeviceIdType.MESH
BS = 128
NLB = 8
NOCC = 1920
NAUX = 32
NAT = 16
NRB = 128
DEPTH = NLB * BS
SIDE = 4
SCALE = 1.0 / (NAUX * NOCC)
SENDS = (1, 3, 2)
ORDER = (2, 3, 1)
TURNS = (2, 3, 1)
STEP = 640
COLUMNS = ((0, 512), (512, 512), (1024, 512), (1536, 384))
PAIRS = [(d, 0) for d in (0,) + ORDER] + [(d, e) for d in (0,) + ORDER for e in TURNS]
EARLY, LATE = PAIRS[:14], PAIRS[14:]


def place():
    a, o = lax.axis_index("aux"), lax.axis_index("orb")
    return a // SIDE, a % SIDE, o // 2, o % 2


def tile_of(x, z, dx, dz):
    return (x + SIDE - dx) % SIDE * SIDE + (z + SIDE - dz) % SIDE


def fill(p, dx, dz, x, z, fin_ref, mask_ref, lhs, k):
    keep = mask_ref[pl.ds(tile_of(x, z, dx, dz), 1), :]
    rows = pl.ds(pl.multiple_of(k * BS, BS), BS)
    for j in range(NLB):
        block = fin_ref[p, dx, dz, j].astype(jnp.float32) * keep[:, j * BS : (j + 1) * BS]
        lhs[rows, j * BS : (j + 1) * BS] = block.astype(jnp.bfloat16)


def gram(half):
    return lax.dot_general(half, half, (((1,), (1,)), ((), ())), preferred_element_type=jnp.float32)


def gather_kernel(
    ints, panel, screen, owner, hv, fin, dens, mask, kacc,
    xa, zb, prcv, scr, own, lhs, s_one, r_one, s_two, r_fin, s_pan, r_pan, l_sem, d_sem,
):
    x, z, y, c = place()
    o = y * 2 + c

    def at_xz(dx, dz):
        return ((x + dx) % SIDE * SIDE + (z + dz) % SIDE, o)

    def at_orb(dy, dc):
        return (x * SIDE + z, (y + dy) % SIDE * 2 + (c + dc) % 2)

    def send(src, dst, ss, rs, to):
        return pltpu.make_async_remote_copy(
            src_ref=src, dst_ref=dst, send_sem=ss, recv_sem=rs, device_id=to, device_id_type=MESH
        )

    barrier = pltpu.get_barrier_semaphore()
    for d in (1, 2, 3):
        for to in (at_xz(d, 0), at_xz(0, d), at_orb(d, 0)):
            pl.semaphore_signal(barrier, inc=1, device_id=to, device_id_type=MESH)
    pl.semaphore_signal(barrier, inc=1, device_id=at_orb(0, 1), device_id_type=MESH)
    pl.semaphore_wait(barrier, 10)

    relay_a, relay_b = {}, {}
    for d in SENDS:
        relay_a[d] = send(ints.at[0, (x + d) % SIDE], xa.at[d - 1], s_one.at[0], r_one.at[0, d - 1], at_xz(d, 0))
        relay_b[d] = send(ints.at[1, :, (z + d) % SIDE], zb.at[d - 1], s_one.at[1], r_one.at[1, d - 1], at_xz(0, d))
        relay_a[d].start()
        relay_b[d].start()
    panels = {d: send(panel.at[0], prcv.at[o], s_pan.at[0], r_pan.at[0, d], at_orb(d, 0)) for d in ORDER}
    for d in ORDER:
        panels[d].start()
    direct = []
    for e in TURNS:
        direct.append(send(ints.at[0, x, (z + e) % SIDE], fin.at[0, 0, e], s_two.at[0], r_fin.at[0, e - 1], at_xz(0, e)))
        direct.append(send(ints.at[1, (x + e) % SIDE, z], fin.at[1, e, 0], s_two.at[1], r_fin.at[0, e - 1], at_xz(e, 0)))
    for copy in direct:
        copy.start()
    mine = [
        pltpu.make_async_copy(ints.at[0, x, z], fin.at[0, 0, 0], l_sem.at[0]),
        pltpu.make_async_copy(ints.at[1, x, z], fin.at[1, 0, 0], l_sem.at[1]),
        pltpu.make_async_copy(panel.at[0], prcv.at[o], l_sem.at[2]),
    ]
    row = o * SIDE * SIDE + x * SIDE + z
    masks = pltpu.make_async_copy(screen, scr, l_sem.at[3])
    masks.start()
    owners = pltpu.make_async_copy(owner, own, l_sem.at[4])
    owners.start()
    for copy in mine:
        copy.start()
    shared = {0: send(panel.at[0], prcv.at[o], s_pan.at[1], r_pan.at[1, 0], at_orb(0, 1))}
    shared[0].start()

    masks.wait()
    pick = lax.broadcasted_iota(jnp.int32, (NAT, NLB, NRB), 2) == row
    kept = jnp.sum(jnp.where(pick, scr[...], 0).astype(jnp.float32), axis=2)
    wide = lax.broadcasted_iota(jnp.int32, (NLB, DEPTH), 1) // BS == lax.broadcasted_iota(jnp.int32, (NLB, DEPTH), 0)
    mask[...] = jnp.dot(kept, wide.astype(jnp.float32), preferred_element_type=jnp.float32)
    kacc[...] = jnp.zeros_like(kacc)

    for d in ORDER:
        panels[d].wait_recv()
        slot = (y + SIDE - d) % SIDE * 2 + c
        shared[d] = send(prcv.at[slot], prcv.at[slot], s_pan.at[1], r_pan.at[1, d], at_orb(0, 1))
        shared[d].start()

    second = {}
    for d in ORDER:
        relay_a[d].wait_recv()
        relay_b[d].wait_recv()
        for e in TURNS:
            second[0, d, e] = send(xa.at[d - 1, (z + e) % SIDE], fin.at[0, d, e], s_two.at[0], r_fin.at[d, e - 1], at_xz(0, e))
            second[1, d, e] = send(zb.at[d - 1, (x + e) % SIDE], fin.at[1, e, d], s_two.at[1], r_fin.at[d, e - 1], at_xz(e, 0))
            second[0, d, e].start()
            second[1, d, e].start()
        mine.append(pltpu.make_async_copy(xa.at[d - 1, z], fin.at[0, d, 0], d_sem.at[0, d - 1]))
        mine.append(pltpu.make_async_copy(zb.at[d - 1, x], fin.at[1, 0, d], d_sem.at[1, d - 1]))
        mine[-2].start()
        mine[-1].start()

    for d in range(SIDE):
        shared[d].wait_recv()
    for copy in mine:
        copy.wait()
    owners.wait()
    for j in range(NLB):
        dens[j * BS : (j + 1) * BS, :] = prcv[own[j]]

    def pair(d, e):
        both = fin.at[0, pl.ds(0, 2), 0]
        send(both, both, s_one.at[0], r_fin.at[d, e - 1], at_xz(1, 0)).wait_recv()

    def work(d, e):
        spots = [tile_of(x, z, d, e) * 2, tile_of(x, z, e, d) * 2 + 1]
        fill(0, d, e, x, z, fin, mask, lhs, 0)
        fill(1, e, d, x, z, fin, mask, lhs, 1)
        for at, width in COLUMNS:
            product = jnp.dot(lhs[...], dens[:, at : at + width], preferred_element_type=jnp.float32)
            product = product.astype(jnp.bfloat16)
            for p in range(2):
                hv[pl.ds(spots[p], 1), :, at : at + width] = product[p * BS : (p + 1) * BS].reshape(1, BS, width)
        for p in range(2):
            kacc[...] += gram(hv[pl.ds(spots[p], 1)].reshape(BS, NOCC))

    def step(g, _):
        d, e = pair_at(g)

        @pl.when(g >= SIDE)
        def _():
            pair(d, e)

        work(d, e)
        return 0

    lax.fori_loop(0, len(EARLY), step, 0)
    for whole, sem in (
        (xa, s_one.at[0]), (zb, s_one.at[1]), (xa, s_two.at[0]), (zb, s_two.at[1]),
        (prcv.at[pl.ds(0, 3)], s_pan.at[0]), (prcv.at[pl.ds(0, 4)], s_pan.at[1]),
    ):
        send(whole, whole, sem, r_fin.at[0, 0], at_xz(1, 0)).wait_send()
    for d, e in LATE:
        pair(d, e)


def pair_at(g):
    h = lax.max(g - SIDE, 0)
    first = g < SIDE
    return pick(jnp.where(first, g, h // 3), (0,) + ORDER), jnp.where(first, 0, pick(h % 3, TURNS))


def pick(i, values):
    result = values[-1]
    for k in range(len(values) - 2, -1, -1):
        result = jnp.where(i == k, values[k], result)
    return result


def finish_kernel(hv, fin, dens, mask, kacc, halves, kblocks, lhs, late, kout, sem, k_sem):
    x, z, y, c = place()
    def out(source, spot, count):
        pltpu.make_async_copy(source, halves.at[0, pl.ds(spot, count)], sem).start()

    left = [unit for d, e in LATE for unit in ((0, d, e), (1, e, d))]
    whole = [dx for dx in range(SIDE) if all(dx != unit[1] for unit in left)]
    for dx in whole:
        spot = (x + SIDE - dx) % SIDE * SIDE * 2
        out(hv.at[pl.ds(spot, 2 * SIDE)], spot, 2 * SIDE)
    rest = []
    for dx in range(SIDE):
        for dz in range(SIDE):
            ready = [p for p in range(2) if (p, dx, dz) not in left]
            if ready and dx not in whole:
                rest.append((tile_of(x, z, dx, dz) * 2 + ready[0], len(ready)))
    for spot, count in rest:
        out(hv.at[pl.ds(spot, count)], spot, count)

    def unit(k):
        d, e, p = pick(k // 2, [pair[0] for pair in LATE]), pick(k // 2, [pair[1] for pair in LATE]), k % 2
        return p, (1 - p) * d + p * e, (1 - p) * e + p * d

    def stage(k, _):
        p, dx, dz = unit(k)
        fill(p, dx, dz, x, z, fin, mask, lhs, k)
        return 0

    def column(i, _):
        at = pl.multiple_of(i * STEP, STEP)
        product = jnp.dot(lhs[...], dens[:, pl.ds(at, STEP)], preferred_element_type=jnp.float32)
        late[:, :, pl.ds(at, STEP)] = product.astype(jnp.bfloat16).reshape(len(left), BS, STEP)
        return 0

    lax.fori_loop(0, len(left), stage, 0)
    lax.fori_loop(0, NOCC // STEP, column, 0)
    for k in range(len(left)):
        p, dx, dz = unit(k)
        out(late.at[pl.ds(k, 1)], tile_of(x, z, dx, dz) * 2 + p, 1)
    total = lax.fori_loop(0, len(left), lambda k, total: total + gram(late[k]), kacc[...])
    kout[0] = total * SCALE
    last = pltpu.make_async_copy(kout, kblocks, k_sem)
    last.start()
    pltpu.make_async_copy(hv, halves.at[0], sem).wait()
    last.wait()


def shards(integrals, panels, screen, owner_map):
    piece = (NLB, BS, BS)
    vmem = pl.BlockSpec(memory_space=pltpu.VMEM)
    hbm = pl.BlockSpec(memory_space=pl.ANY)
    dma = pltpu.SemaphoreType.DMA
    bf16, f32 = jnp.bfloat16, jnp.float32
    ints = integrals.reshape((2, SIDE, SIDE) + piece)
    between = pl.pallas_call(
        gather_kernel,
        name="gather",
        out_shape=[
            pltpu.VMEM((NAUX, BS, NOCC), bf16),
            pltpu.VMEM((2, SIDE, SIDE) + piece, bf16),
            pltpu.VMEM((DEPTH, NOCC), bf16),
            pltpu.VMEM((NAT, DEPTH), f32),
            pltpu.VMEM((BS, BS), f32),
        ],
        in_specs=[hbm] * 4,
        out_specs=[vmem] * 5,
        scratch_shapes=[
            pltpu.VMEM((3, SIDE) + piece, bf16),
            pltpu.VMEM((3, SIDE) + piece, bf16),
            pltpu.VMEM((NLB, BS, NOCC), bf16),
            pltpu.VMEM((NAT, NLB, NRB), jnp.int32),
            pltpu.SMEM((NLB,), jnp.int32),
            pltpu.VMEM((2 * BS, DEPTH), bf16),
            dma((2,)),
            dma((2, 3)),
            dma((2,)),
            dma((4, 3)),
            dma((2,)),
            dma((2, 4)),
            dma((5,)),
            dma((2, 3)),
        ],
        compiler_params=pltpu.CompilerParams(collective_id=0, has_side_effects=True, vmem_limit_bytes=24 << 20),
        cost_estimate=pl.CostEstimate(flops=16 << 30, bytes_accessed=24 << 20, transcendentals=0),
    )(*(pltpu.with_memory_space_constraint(v, pltpu.HBM) for v in (ints, panels, screen.transpose(0, 2, 1), owner_map)))
    return pl.pallas_call(
        finish_kernel,
        name="finish",
        out_shape=[
            pltpu.HBM((1, NAUX, BS, NOCC), bf16),
            pltpu.HBM((1, BS, BS), f32),
        ],
        in_specs=[vmem] * 5,
        out_specs=[hbm, hbm],
        scratch_shapes=[
            pltpu.VMEM((2 * len(LATE) * BS, DEPTH), bf16),
            pltpu.VMEM((2 * len(LATE), BS, NOCC), bf16),
            pltpu.VMEM((1, BS, BS), f32),
            dma(()),
            dma(()),
        ],
        compiler_params=pltpu.CompilerParams(vmem_limit_bytes=24 << 20),
        cost_estimate=pl.CostEstimate(flops=2 << 30, bytes_accessed=16 << 20, transcendentals=0),
    )(*(pltpu.with_memory_space_constraint(v, pltpu.VMEM) for v in between))


def solution(mesh):
    placed = (P("aux", "orb", None, None, None), P("orb", None, None), P(), P())
    return jax.shard_map(
        shards,
        mesh=mesh,
        in_specs=placed,
        out_specs=(P(("orb", "aux"), None, None, None), P(("orb", "aux"), None, None)),
        check_vma=False,
    )
```
